32 devices in a mesh: runs: 2 (over x), tile: 16 (over z, y, core).
Axes of the slice: x: 2, y: 2, z: 4, core: 2. Of those that a mesh axis runs over, the one named last changes fastest.
Arguments:
- image_stack: bfloat16 [64, 144, 256], P(('runs', 'tile')), parts along dimension 0, may hold values from -6 to 6
- tissue_rows: int32 [64], P(('runs', 'tile')), parts along dimension 0, may hold values from 0 to 12, as said below
- filters: bfloat16 [256, 7744], replicated, may hold values from -24 to 24
- codes_start: bfloat16 [64, 9216], P(('runs', 'tile')), parts along dimension 0, may hold values from -4 to 4
- duals_start: bfloat16 [64, 9216], P(('runs', 'tile')), parts along dimension 0, may hold values from -2 to 2
Outputs:
- sparse_codes: float32 [64, 9216], P(('runs', 'tile')), parts along dimension 0
- dual_state: float32 [64, 9216], P(('runs', 'tile')), parts along dimension 0
- new_filters: bfloat16 [512, 7744], P('runs'), parts along dimension 0
The draws below stay inside these ranges and needn't reach their ends.
There are 2 independent parts, one for each index of `runs`. The reference program is written for one: setup_inputs(seed, part) draws one part's arguments, and reference() takes and returns one part's arrays. A program takes and returns all parts, laid end to end along the dimension named above; an argument that names none is the same for every part. Nothing has to cross between parts.
Inputs may be any that keep to these rules, and one draw needn't show every extreme that they name: `tissue_rows`: each device holds 2 slots; a slot is occupied when its row count is positive, and a device's occupied slots come first. Devices 2j and 2j + 1 of the tile axis hold exactly 2 occupied slots together, and some pair has all of them on one device. The first slot of a device with an occupied slot has all 12 rows.
All inputs are finite; a program needn't handle non-finite values.
Results may differ from the reference program's by a relative error of at most 0.03.
Values may be sent and summed in bfloat16 or wider, within the bound.
A program may use at most 128 MiB of HBM per device.

```python
import math
import jax
import jax.numpy as jnp
from jax import lax

M = 64
C = 256
K = 11
SIDE = 12
SLOTS = 2
ITERS = 2
TILES = 32


def draw_tissue_rows(key, part):
    devices = TILES // SLOTS
    pairs = devices // 2
    pair_fill = jax.random.randint(jax.random.fold_in(key, 11), (pairs,), 0, SLOTS + 1)
    pair_fill = jnp.where(jnp.arange(pairs) == 0, SLOTS, pair_fill)
    occupied = jnp.stack([pair_fill, SLOTS - pair_fill], axis=1).reshape(devices)
    heights = jax.random.randint(jax.random.fold_in(key, 12), (devices, SLOTS), 1, SIDE + 1)
    slot_index = jnp.arange(SLOTS)[None, :]
    heights = jnp.where(slot_index == 0, SIDE, heights)
    filled = jnp.where(slot_index < occupied[:, None], heights, 0)
    return filled.reshape(TILES).astype(jnp.int32)


def draw_filters(key, part):
    channel = jnp.arange(C, dtype=jnp.float32)[:, None]
    ramp = 1.0 + 2.0 * channel / (C - 1)
    base = jnp.clip(jax.random.normal(jax.random.fold_in(key, 23), (C, K * K * M), jnp.float32), -6.0, 6.0)
    return (base * ramp).astype(jnp.bfloat16)


def level_of(key, extent, split, smallest, high):
    level = 1.0
    for axis_at, parts in split:
        steps = jax.random.uniform(jax.random.fold_in(jax.random.fold_in(key, 6), axis_at), (parts,), jnp.float32, smallest / len(split), high / len(split))
        level = level * jnp.repeat(jnp.exp(steps), extent[axis_at] // parts).reshape((-1,) + (1,) * (len(extent) - 1 - axis_at))
    return level


def noise(rng, shape, width, limit, split=(), kind=jnp.bfloat16):
    loudness = level_of(rng, shape, split, -0.22, 0.18) if split else 1.0
    values = jax.random.normal(rng, shape, jnp.float32) * width * loudness
    return jnp.minimum(jnp.maximum(values, -limit), limit).astype(kind)


def setup_inputs(seed: int = 0, part: int = 0) -> dict:
    splits = jax.random.split(jax.random.key(seed), 6)
    part_splits = jax.random.split(jax.random.fold_in(splits[5], part), 6)
    return {
        "image_stack": noise(part_splits[0], (TILES, SIDE * SIDE, C), 1.0, 6.0, ((0, 16),)),
        "tissue_rows": draw_tissue_rows(jax.random.fold_in(jax.random.fold_in(splits[5], part), 71), part),
        "filters": draw_filters(jax.random.fold_in(splits[5], 71), part),
        "codes_start": noise(part_splits[3], (TILES, SIDE * SIDE * M), 1.0, 4.0, ((0, 16),)),
        "duals_start": noise(part_splits[4], (TILES, SIDE * SIDE * M), 0.3, 2.0, ((0, 16),)),
    }


PENALTY = 10.0
SPARSITY = 2.0
EPSILON = 1e-05
RELAX = 1.8

def patches_of(code_maps):
    number = code_maps.shape[0]
    margin = (K - 1) // 2
    padded = jnp.pad(code_maps, ((0, 0), (margin, margin), (margin, margin), (0, 0)))
    columns = [padded[:, row_off:row_off + SIDE, col_off:col_off + SIDE, :] for row_off in range(K) for col_off in range(K)]
    return jnp.stack(columns, axis=3).reshape(number * SIDE * SIDE, K * K * M)

def fold_back(correlation):
    number = correlation.shape[0] // (SIDE * SIDE)
    margin = (K - 1) // 2
    shaped = correlation.reshape(number, SIDE, SIDE, K * K, M)
    summed = jnp.zeros((number, SIDE, SIDE, M), jnp.float32)
    for row_off in range(K):
        for col_off in range(K):
            top = 2 * margin - row_off
            left = 2 * margin - col_off
            piece = shaped[:, :, :, row_off * K + col_off, :].astype(jnp.float32)
            padded = jnp.pad(piece, ((0, 0), (margin, margin), (margin, margin), (0, 0)))
            summed = summed + padded[:, top:top + SIDE, left:left + SIDE, :]
    return summed.reshape(number, SIDE * SIDE, M)

def normalized(moved, squares):
    rows_here = moved.shape[0]
    norms = jnp.sqrt(squares / (C * K * K) + EPSILON)
    return (moved.reshape(rows_here, K * K, M) / norms).reshape(rows_here, K * K * M).astype(jnp.bfloat16)

def admm_update(codes_now, duals_now, gradient):
    primal = codes_now - duals_now - gradient / PENALTY
    relaxed = RELAX * primal + (1.0 - RELAX) * codes_now
    merged = relaxed + duals_now
    shrunk = jnp.sign(merged) * jnp.maximum(jnp.abs(merged) - SPARSITY / PENALTY, 0.0)
    return (shrunk, duals_now + relaxed - shrunk)

def reference(image_stack, tissue_rows, filters, codes_start, duals_start):
    tile_count = image_stack.shape[0]
    pixels = SIDE * SIDE
    factor = 1.0 / math.sqrt(K * K * M)
    stride = 0.5 * math.sqrt(K * K * M / (pixels * tile_count))
    blocks = tile_count // SLOTS
    tissue = (jnp.arange(pixels)[None, :] // SIDE < tissue_rows[:, None]).astype(jnp.float32)
    tissue_blocks = tissue.reshape(blocks, SLOTS * pixels, 1)
    image_blocks = image_stack.reshape(blocks, SLOTS * pixels, C)
    codes_now = codes_start.astype(jnp.float32).reshape(tile_count, pixels, M)
    duals_now = duals_start.astype(jnp.float32).reshape(tile_count, pixels, M)
    summed = jnp.zeros((C, K * K * M), jnp.float32)
    for iteration in range(ITERS):
        code_blocks = codes_now.reshape(blocks, SLOTS, SIDE, SIDE, M)

        def block_step(total, entry_item):
            images, tissue_block, code_block = entry_item
            patches = patches_of(code_block.astype(jnp.bfloat16))
            rebuilt = jnp.dot(patches, filters.T, preferred_element_type=jnp.float32) * factor
            residual = (tissue_block * (rebuilt - images.astype(jnp.float32))).astype(jnp.bfloat16)
            block_term = lax.dot_general(residual, patches, (((0,), (0,)), ((), ())), preferred_element_type=jnp.float32) * factor
            correlation = (jnp.dot(residual, filters, preferred_element_type=jnp.float32) * factor).astype(jnp.bfloat16)
            return (total + block_term, fold_back(correlation))
        summed, gradients = lax.scan(block_step, jnp.zeros((C, K * K * M), jnp.float32), (image_blocks, tissue_blocks, code_blocks))
        gradient = gradients.reshape(tile_count, pixels, M)
        codes_now, duals_now = admm_update(codes_now, duals_now, gradient)
    moved = filters.astype(jnp.float32) - stride * summed
    squares = lax.optimization_barrier(jnp.sum((moved * moved).reshape(C, K * K, M), axis=(0, 1)))
    current = normalized(moved, squares)
    return (codes_now.reshape(tile_count, pixels * M), duals_now.reshape(tile_count, pixels * M), current)
```

```python
import math

import jax
import jax.numpy as jnp
from jax import lax
from jax.experimental import pallas as pl
from jax.experimental.pallas import tpu as pltpu
from jax.sharding import PartitionSpec as P

M = 64
C = 256
K = 11
SIDE = 12
JP = 16
PAIR = 2 * K * M
LAST = K * M
COLS = K * K * M
BLOCKS = PAIR // 128
FACTOR = 1.0 / math.sqrt(K * K * M)

PENALTY = 10.0
SPARSITY = 2.0
EPSILON = 1e-05
RELAX = 1.8

F32 = jnp.float32
BF16 = jnp.bfloat16


def put_codes(dpad, codes):
    both = jnp.concatenate([codes, codes], axis=-1)
    dpad[5 : 5 + SIDE, :, 6 : 6 + SIDE, 0:M] = both[..., 0:M]
    dpad[5 : 5 + SIDE, :, 5 : 5 + SIDE, M : 2 * M] = both[..., M : 2 * M]


def build_taps(dpad, taps):
    slots = dpad.shape[1]
    rows = 22 * slots * JP
    for q in range(BLOCKS):
        if q < 5:
            block = dpad[0:22, :, 2 * q + 1 : 2 * q + 1 + JP, :]
        elif q > 5:
            start = 2 * (q - 6) + 2
            block = dpad[1:23, :, start : start + JP, :]
        else:
            low = dpad[0:22, :, 11 : 11 + JP, :]
            high = dpad[1:23, :, 0:JP, :]
            lane = lax.broadcasted_iota(jnp.int32, low.shape, 3)
            block = jnp.where(lane < M, low, high)
        taps[:, q * 128 : (q + 1) * 128] = block.reshape(rows, 128).astype(BF16)


def rebuild(taps, f_ref, slots):
    rows = SIDE * slots * JP
    total = None
    for p in range(6):
        width = PAIR if p < 5 else LAST
        at = p * 2 * slots * JP
        part = lax.dot_general(
            taps[at : at + rows, 0:width],
            f_ref[:, p * PAIR : p * PAIR + width],
            (((1,), (1,)), ((), ())),
            preferred_element_type=F32,
        )
        total = part if total is None else total + part
    return total


def fill_tail(f_ref, ftail):
    ftail[...] = jnp.zeros_like(ftail)
    ftail[:, 0:192] = f_ref[:, COLS - 192 : COLS]


def code_gradient(rpad, f_ref, ftail, zpad, slots):
    rows = 13 * slots * JP
    step = slots * JP
    for n in range(6):
        width = 256 if n < 5 else 128
        acc = None
        for p in range(6):
            at = (10 - 2 * p) * step
            if p < 5:
                piece = f_ref[:, p * PAIR + n * 256 : p * PAIR + n * 256 + width]
            elif n < 2:
                piece = f_ref[:, p * PAIR + n * 256 : p * PAIR + n * 256 + width]
            elif n == 2:
                piece = ftail[...]
            else:
                continue
            part = jnp.dot(rpad[at : at + rows, :], piece, preferred_element_type=F32)
            acc = part if acc is None else acc + part
        for h in range(width // 128):
            zpad[2 * n + h, :, :, 8:24, :] = acc[:, h * 128 : (h + 1) * 128].reshape(
                13, slots, JP, 128
            )
    total = None
    for q in range(BLOCKS):
        if q < 5:
            part = zpad[q, 1:13, :, 12 - 2 * q : 36 - 2 * q, :]
        elif q > 5:
            start = 11 - 2 * (q - 6)
            part = zpad[q, 0:12, :, start : start + 24, :]
        else:
            low = zpad[q, 1:13, :, 2:26, :]
            high = zpad[q, 0:12, :, 13:37, :]
            lane = lax.broadcasted_iota(jnp.int32, low.shape, 3)
            part = jnp.where(lane < M, low, high)
        total = part if total is None else total + part
    zpad[0, 0:12, :, 0:24, :] = total
    low = zpad[0, 0:12, :, 1 : 1 + JP, 0:M]
    high = zpad[0, 0:12, :, 0:JP, M : 2 * M]
    return (low + high) * FACTOR


def admm_update(codes_now, duals_now, gradient):
    primal = codes_now - duals_now - gradient / PENALTY
    relaxed = RELAX * primal + (1.0 - RELAX) * codes_now
    merged = relaxed + duals_now
    level = SPARSITY / PENALTY
    shrunk = jnp.where(
        merged > level, merged - level, jnp.where(merged < -level, merged + level, 0.0)
    )
    return shrunk, duals_now + relaxed - shrunk


def tissue_of(rows_ref, shape):
    row = lax.broadcasted_iota(jnp.int32, shape, 0)
    slot = lax.broadcasted_iota(jnp.int32, shape, 1)
    col = lax.broadcasted_iota(jnp.int32, shape, 2)
    height = jnp.full(shape, 0, jnp.int32)
    for s in range(shape[1]):
        height = jnp.where(slot == s, rows_ref[s], height)
    return (row < height) & (col < SIDE), height > 0


def first_kernel(
    rows_ref, f_ref, img_ref, codes_ref, duals_ref, pay_ref, codes_out, duals_out,
    dpad, taps, rpad, ftail, zpad, stage
):
    slots = img_ref.shape[1]
    rows = SIDE * slots * JP
    lead = 6 * slots * JP
    dpad[...] = jnp.zeros_like(dpad)
    rpad[...] = jnp.zeros_like(rpad)
    zpad[...] = jnp.zeros_like(zpad)
    fill_tail(f_ref, ftail)
    inside, occupied = tissue_of(rows_ref, (SIDE, slots, JP, C))
    codes = codes_ref[...].astype(F32)
    duals = duals_ref[...].astype(F32)
    images = img_ref[...].astype(F32)

    def residual_of(values):
        put_codes(dpad, values[:, :, 0:SIDE, :])
        build_taps(dpad, taps)
        rebuilt = rebuild(taps, f_ref, slots).reshape(SIDE, slots, JP, C) * FACTOR
        return jnp.where(inside, rebuilt - images, 0.0)

    residual = residual_of(codes)
    rpad[lead : lead + rows, :] = residual.reshape(rows, C).astype(BF16)
    gradient = code_gradient(rpad, f_ref, ftail, zpad, slots)
    codes, duals = admm_update(codes, duals, gradient)
    codes_out[...] = codes
    duals_out[...] = duals
    residual = residual_of(codes)
    stage[...] = residual
    held = jnp.where(occupied[..., 0:M], codes, 0.0)
    for k in range(3):
        stage[:, :, SIDE:JP, k * M : (k + 1) * M] = held[:, :, 4 * k : 4 * k + 4, :]
    pay_ref[...] = stage[...].astype(BF16)


def second_kernel(f_ref, pay_ref, codes_ref, duals_ref, codes_out, duals_out, rpad, ftail, zpad):
    slots = pay_ref.shape[1]
    rows = SIDE * slots * JP
    lead = 6 * slots * JP
    rpad[...] = jnp.zeros_like(rpad)
    zpad[...] = jnp.zeros_like(zpad)
    fill_tail(f_ref, ftail)
    payload = pay_ref[...].astype(F32)
    col = lax.broadcasted_iota(jnp.int32, payload.shape, 2)
    residual = jnp.where(col < SIDE, payload, 0.0)
    rpad[lead : lead + rows, :] = residual.reshape(rows, C).astype(BF16)
    gradient = code_gradient(rpad, f_ref, ftail, zpad, slots)
    codes, duals = admm_update(codes_ref[...], duals_ref[...], gradient)
    codes_out[...] = codes
    duals_out[...] = duals


def dictionary_kernel(stride, f_ref, all_ref, new_ref, dpad, taps, stage, total):
    at = pl.program_id(0)
    group = all_ref.shape[0]
    rows = SIDE * group * JP

    @pl.when(at == 0)
    def _():
        dpad[...] = jnp.zeros_like(dpad)
        total[...] = jnp.zeros_like(total)

    for d in range(0, group, 2):
        for k in range(2):
            stage[:, d + k, :, :] = all_ref[d, :, k, :, :].astype(F32) + all_ref[
                d + 1, :, 1 - k, :, :
            ].astype(F32)
    for k in range(3):
        lanes = slice(k * M, (k + 1) * M)
        codes = stage[:, :, SIDE:JP, lanes]
        both = jnp.concatenate([codes, codes], axis=-1)
        dpad[5 : 5 + SIDE, :, 6 + 4 * k : 10 + 4 * k, 0:M] = both[..., 0:M]
        dpad[5 : 5 + SIDE, :, 5 + 4 * k : 9 + 4 * k, M : 2 * M] = both[..., M : 2 * M]
    build_taps(dpad, taps)
    values = stage[...]
    col = lax.broadcasted_iota(jnp.int32, values.shape, 2)
    turned = jnp.where(col < SIDE, values, 0.0).reshape(rows, C).T.astype(BF16)
    for p in range(6):
        width = PAIR if p < 5 else LAST
        start = p * 2 * group * JP
        total[:, p * PAIR : p * PAIR + width] += jnp.dot(
            turned, taps[start : start + rows, 0:width], preferred_element_type=F32
        )

    @pl.when(at == pl.num_programs(0) - 1)
    def _():
        squares = jnp.zeros((C, 128), F32)
        for q in range(COLS // 128 + 1):
            width = min(128, COLS - q * 128)
            lanes = slice(q * 128, q * 128 + width)
            moved = f_ref[:, lanes].astype(F32) - (stride * FACTOR) * total[:, lanes]
            total[:, lanes] = moved
            if width == 128:
                squares = squares + moved * moved
        tail = jnp.sum(moved * moved, axis=0, keepdims=True)
        sums = jnp.sum(squares, axis=0, keepdims=True)
        each = sums[:, 0:M] + sums[:, M : 2 * M] + tail
        inverse = 1.0 / jnp.sqrt(each / (C * K * K) + EPSILON)
        wide = jnp.concatenate([inverse, inverse], axis=-1)
        for q in range(COLS // 128 + 1):
            width = min(128, COLS - q * 128)
            lanes = slice(q * 128, q * 128 + width)
            new_ref[:, lanes] = (total[:, lanes] * wide[:, 0:width]).astype(BF16)


def in_vmem():
    return pl.BlockSpec(memory_space=pltpu.VMEM)


LIMIT = 56 * 1024 * 1024


def cost(flops):
    return pl.CostEstimate(flops=flops, bytes_accessed=8 * 1024 * 1024, transcendentals=0)


def local(image_stack, tissue_rows, filters, codes_start, duals_start):
    slots = image_stack.shape[0]
    groups = lax.axis_size("tile")
    stride = 0.5 * math.sqrt(COLS / (SIDE * SIDE * slots * groups))

    def arranged(array, width):
        shaped = array.reshape(slots, SIDE, SIDE, width).transpose(1, 0, 2, 3)
        return jnp.pad(shaped, ((0, 0), (0, 0), (0, JP - SIDE), (0, 0)))

    state = jax.ShapeDtypeStruct((SIDE, slots, JP, M), F32)
    one_product = 2 * SIDE * SIDE * slots * C * COLS
    back = [
        pltpu.VMEM((23 * slots * JP, C), BF16),
        pltpu.VMEM((C, 256), BF16),
        pltpu.VMEM((BLOCKS, 13, slots, 40, 128), F32),
    ]
    payload, codes_mid, duals_mid = pl.pallas_call(
        first_kernel,
        out_shape=(jax.ShapeDtypeStruct((SIDE, slots, JP, C), BF16), state, state),
        in_specs=[pl.BlockSpec(memory_space=pltpu.SMEM)] + [in_vmem()] * 4,
        out_specs=(in_vmem(),) * 3,
        scratch_shapes=[
            pltpu.VMEM((23, slots, 32, 128), F32),
            pltpu.VMEM((22 * slots * JP, PAIR), BF16),
        ]
        + back
        + [pltpu.VMEM((SIDE, slots, JP, C), F32)],
        compiler_params=pltpu.CompilerParams(vmem_limit_bytes=LIMIT),
        cost_estimate=cost(3 * one_product),
        name="first_pass",
    )(
        tissue_rows,
        filters,
        arranged(image_stack, C),
        arranged(codes_start, M),
        arranged(duals_start, M),
    )
    everyone = lax.all_gather(payload, "tile", axis=0)
    codes, duals = pl.pallas_call(
        second_kernel,
        out_shape=(state, state),
        in_specs=[in_vmem()] * 4,
        out_specs=(in_vmem(),) * 2,
        scratch_shapes=back,
        compiler_params=pltpu.CompilerParams(vmem_limit_bytes=LIMIT),
        cost_estimate=cost(one_product),
        name="second_codes",
    )(filters, payload, codes_mid, duals_mid)
    group = 4 if groups % 4 == 0 else 2
    new_filters = pl.pallas_call(
        lambda *refs: dictionary_kernel(stride, *refs),
        grid=(groups // group,),
        out_shape=jax.ShapeDtypeStruct((C, COLS), BF16),
        in_specs=[
            pl.BlockSpec((C, COLS), lambda g: (0, 0), pipeline_mode=pl.Buffered(1)),
            pl.BlockSpec((group, SIDE, slots, JP, C), lambda g: (g, 0, 0, 0, 0)),
        ],
        out_specs=pl.BlockSpec((C, COLS), lambda g: (0, 0), pipeline_mode=pl.Buffered(1)),
        scratch_shapes=[
            pltpu.VMEM((23, group, 32, 128), F32),
            pltpu.VMEM((22 * group * JP, PAIR), BF16),
            pltpu.VMEM((SIDE, group, JP, C), F32),
            pltpu.VMEM((C, COLS), F32),
        ],
        compiler_params=pltpu.CompilerParams(vmem_limit_bytes=LIMIT),
        cost_estimate=cost(groups * one_product // 2),
        name="dictionary",
    )(filters, everyone)

    def flat(array):
        return array[:, :, 0:SIDE, :].transpose(1, 0, 2, 3).reshape(slots, SIDE * SIDE * M)

    return flat(codes), flat(duals), new_filters


def solution(mesh):
    return jax.shard_map(
        local,
        mesh=mesh,
        in_specs=(
            P(("runs", "tile"), None, None),
            P(("runs", "tile")),
            P(),
            P(("runs", "tile"), None),
            P(("runs", "tile"), None),
        ),
        out_specs=(P(("runs", "tile"), None), P(("runs", "tile"), None), P("runs", None)),
        check_vma=False,
    )
```

```python
import math

import jax
import jax.numpy as jnp
from jax import lax
from jax.experimental import pallas as pl
from jax.experimental.pallas import tpu as pltpu
from jax.sharding import PartitionSpec as P

M = 64
C = 256
K = 11
SIDE = 12
JP = 16
PAIR = 2 * K * M
LAST = K * M
COLS = K * K * M
BLOCKS = PAIR // 128
FACTOR = 1.0 / math.sqrt(K * K * M)

PENALTY = 10.0
SPARSITY = 2.0
EPSILON = 1e-05
RELAX = 1.8

F32 = jnp.float32
BF16 = jnp.bfloat16


def put_codes(dpad, codes):
    both = jnp.concatenate([codes, codes], axis=-1)
    dpad[5 : 5 + SIDE, :, 6 : 6 + SIDE, 0:M] = both[..., 0:M]
    dpad[5 : 5 + SIDE, :, 5 : 5 + SIDE, M : 2 * M] = both[..., M : 2 * M]


def build_taps(dpad, taps):
    slots = dpad.shape[1]
    rows = 22 * slots * JP
    for q in range(BLOCKS):
        if q < 5:
            block = dpad[0:22, :, 2 * q + 1 : 2 * q + 1 + JP, :]
        elif q > 5:
            start = 2 * (q - 6) + 2
            block = dpad[1:23, :, start : start + JP, :]
        else:
            low = dpad[0:22, :, 11 : 11 + JP, :]
            high = dpad[1:23, :, 0:JP, :]
            lane = lax.broadcasted_iota(jnp.int32, low.shape, 3)
            block = jnp.where(lane < M, low, high)
        taps[:, q * 128 : (q + 1) * 128] = block.reshape(rows, 128).astype(BF16)


def rebuild(taps, f_ref, slots):
    rows = SIDE * slots * JP
    total = None
    for p in range(6):
        width = PAIR if p < 5 else LAST
        at = p * 2 * slots * JP
        part = lax.dot_general(
            taps[at : at + rows, 0:width],
            f_ref[p * PAIR : p * PAIR + width, :],
            (((1,), (0,)), ((), ())),
            preferred_element_type=F32,
        )
        total = part if total is None else total + part
    return total


def fill_tail(f_ref, ftail):
    ftail[...] = jnp.zeros_like(ftail)
    ftail[0:192, :] = f_ref[COLS - 192 : COLS, :]


def code_gradient(rpad, f_ref, ftail, zpad, slots):
    rows = 13 * slots * JP
    step = slots * JP
    for n in range(6):
        width = 256 if n < 5 else 128
        acc = None
        for p in range(6):
            at = (10 - 2 * p) * step
            if p < 5 or n < 2:
                piece = f_ref[p * PAIR + n * 256 : p * PAIR + n * 256 + width, :]
            elif n == 2:
                piece = ftail[...]
            else:
                continue
            part = lax.dot_general(
                rpad[at : at + rows, :],
                piece,
                (((1,), (1,)), ((), ())),
                preferred_element_type=F32,
            )
            acc = part if acc is None else acc + part
        for h in range(width // 128):
            zpad[2 * n + h, :, :, 8:24, :] = acc[:, h * 128 : (h + 1) * 128].reshape(
                13, slots, JP, 128
            )
    total = None
    for q in range(BLOCKS):
        if q < 5:
            part = zpad[q, 1:13, :, 12 - 2 * q : 36 - 2 * q, :]
        elif q > 5:
            start = 11 - 2 * (q - 6)
            part = zpad[q, 0:12, :, start : start + 24, :]
        else:
            low = zpad[q, 1:13, :, 2:26, :]
            high = zpad[q, 0:12, :, 13:37, :]
            lane = lax.broadcasted_iota(jnp.int32, low.shape, 3)
            part = jnp.where(lane < M, low, high)
        total = part if total is None else total + part
    zpad[0, 0:12, :, 0:24, :] = total
    low = zpad[0, 0:12, :, 1 : 1 + JP, 0:M]
    high = zpad[0, 0:12, :, 0:JP, M : 2 * M]
    return (low + high) * FACTOR


def admm_update(codes_now, duals_now, gradient):
    primal = codes_now - duals_now - gradient / PENALTY
    relaxed = RELAX * primal + (1.0 - RELAX) * codes_now
    merged = relaxed + duals_now
    level = SPARSITY / PENALTY
    shrunk = jnp.where(
        merged > level, merged - level, jnp.where(merged < -level, merged + level, 0.0)
    )
    return shrunk, duals_now + relaxed - shrunk


def tissue_of(rows_ref, shape):
    row = lax.broadcasted_iota(jnp.int32, shape, 0)
    slot = lax.broadcasted_iota(jnp.int32, shape, 1)
    col = lax.broadcasted_iota(jnp.int32, shape, 2)
    height = jnp.full(shape, 0, jnp.int32)
    for s in range(shape[1]):
        height = jnp.where(slot == s, rows_ref[s], height)
    return (row < height) & (col < SIDE), height > 0


def first_kernel(
    rows_ref, f_ref, img_ref, codes_ref, duals_ref, pay_ref, codes_out, duals_out,
    dpad, taps, rpad, ftail, zpad, stage
):
    slots = img_ref.shape[1]
    rows = SIDE * slots * JP
    lead = 6 * slots * JP
    dpad[...] = jnp.zeros_like(dpad)
    rpad[...] = jnp.zeros_like(rpad)
    zpad[...] = jnp.zeros_like(zpad)
    fill_tail(f_ref, ftail)
    inside, occupied = tissue_of(rows_ref, (SIDE, slots, JP, C))
    codes = codes_ref[...].astype(F32)
    duals = duals_ref[...].astype(F32)
    images = img_ref[...].astype(F32)

    def residual_of(values):
        put_codes(dpad, values[:, :, 0:SIDE, :])
        build_taps(dpad, taps)
        rebuilt = rebuild(taps, f_ref, slots).reshape(SIDE, slots, JP, C) * FACTOR
        return jnp.where(inside, rebuilt - images, 0.0)

    residual = residual_of(codes)
    rpad[lead : lead + rows, :] = residual.reshape(rows, C).astype(BF16)
    gradient = code_gradient(rpad, f_ref, ftail, zpad, slots)
    codes, duals = admm_update(codes, duals, gradient)
    codes_out[...] = codes
    duals_out[...] = duals
    residual = residual_of(codes)
    stage[...] = residual
    held = jnp.where(occupied[..., 0:M], codes, 0.0)
    for k in range(3):
        stage[:, :, SIDE:JP, k * M : (k + 1) * M] = held[:, :, 4 * k : 4 * k + 4, :]
    pay_ref[...] = stage[...].astype(BF16)


def second_kernel(f_ref, pay_ref, codes_ref, duals_ref, codes_out, duals_out, rpad, ftail, zpad):
    slots = pay_ref.shape[1]
    rows = SIDE * slots * JP
    lead = 6 * slots * JP
    rpad[...] = jnp.zeros_like(rpad)
    zpad[...] = jnp.zeros_like(zpad)
    fill_tail(f_ref, ftail)
    payload = pay_ref[...].astype(F32)
    col = lax.broadcasted_iota(jnp.int32, payload.shape, 2)
    residual = jnp.where(col < SIDE, payload, 0.0)
    rpad[lead : lead + rows, :] = residual.reshape(rows, C).astype(BF16)
    gradient = code_gradient(rpad, f_ref, ftail, zpad, slots)
    codes, duals = admm_update(codes_ref[...], duals_ref[...], gradient)
    codes_out[...] = codes
    duals_out[...] = duals


def dictionary_kernel(stride, f_ref, all_ref, new_ref, maps, taps, stage, total):
    at = pl.program_id(0)
    group = all_ref.shape[0]
    row = group * JP
    rows = SIDE * row
    edge = (K - 1) // 2

    @pl.when(at == 0)
    def _():
        maps[...] = jnp.zeros_like(maps)
        taps[...] = jnp.zeros_like(taps)
        total[...] = jnp.zeros_like(total)

    for d in range(0, group, 2):
        for k in range(2):
            stage[:, d + k, :, :] = all_ref[d, :, k, :, :].astype(F32) + all_ref[
                d + 1, :, 1 - k, :, :
            ].astype(F32)
    for k in range(3):
        maps[:, :, 4 * k : 4 * k + 4, :] = stage[:, :, SIDE:JP, k * M : (k + 1) * M]
    col = lax.broadcasted_iota(jnp.int32, (M, row), 1) % JP
    for i in range(SIDE):
        turned = maps[i].reshape(row, M).T
        for b in range(K):
            moved = turned if b == edge else pltpu.roll(turned, (edge - b) % row, 1)
            if b == 0:
                moved = jnp.where(col == 0, 0.0, moved)
            if b == K - 1:
                moved = jnp.where(col == SIDE - 1, 0.0, moved)
            taps[b * M : (b + 1) * M, (i + edge) * row : (i + edge + 1) * row] = moved.astype(BF16)
    values = stage[...]
    place = lax.broadcasted_iota(jnp.int32, values.shape, 2)
    residual = jnp.where(place < SIDE, values, 0.0).reshape(rows, C).astype(BF16)
    for a in range(K):
        total[a * LAST : (a + 1) * LAST, :] += jnp.dot(
            taps[:, a * row : a * row + rows], residual, preferred_element_type=F32
        )

    @pl.when(at == pl.num_programs(0) - 1)
    def _():
        def step(t, squares):
            part = pl.ds(pl.multiple_of(t * M, M), M)
            moved = f_ref[part, :].astype(F32) - (stride * FACTOR) * total[part, :]
            total[part, :] = moved
            return squares + moved * moved

        squares = lax.fori_loop(0, K * K, step, jnp.zeros((M, C), F32), unroll=11)
        sums = jnp.sum(squares, axis=1, keepdims=True)
        inverse = 1.0 / jnp.sqrt(sums / (C * K * K) + EPSILON)

        def scale(t, carry):
            part = pl.ds(pl.multiple_of(t * M, M), M)
            new_ref[part, :] = (total[part, :] * inverse).astype(BF16)
            return carry

        lax.fori_loop(0, K * K, scale, 0, unroll=11)


def in_vmem():
    return pl.BlockSpec(memory_space=pltpu.VMEM)


LIMIT = 56 * 1024 * 1024


def cost(flops):
    return pl.CostEstimate(flops=flops, bytes_accessed=8 * 1024 * 1024, transcendentals=0)


def local(image_stack, tissue_rows, filters, codes_start, duals_start):
    slots = image_stack.shape[0]
    groups = lax.axis_size("tile")
    stride = 0.5 * math.sqrt(COLS / (SIDE * SIDE * slots * groups))

    def arranged(array, width):
        shaped = array.reshape(slots, SIDE, SIDE, width).transpose(1, 0, 2, 3)
        return jnp.pad(shaped, ((0, 0), (0, 0), (0, JP - SIDE), (0, 0)))

    state = jax.ShapeDtypeStruct((SIDE, slots, JP, M), F32)
    one_product = 2 * SIDE * SIDE * slots * C * COLS
    back = [
        pltpu.VMEM((23 * slots * JP, C), BF16),
        pltpu.VMEM((256, C), BF16),
        pltpu.VMEM((BLOCKS, 13, slots, 40, 128), F32),
    ]
    payload, codes_mid, duals_mid = pl.pallas_call(
        first_kernel,
        out_shape=(jax.ShapeDtypeStruct((SIDE, slots, JP, C), BF16), state, state),
        in_specs=[pl.BlockSpec(memory_space=pltpu.SMEM)] + [in_vmem()] * 4,
        out_specs=(in_vmem(),) * 3,
        scratch_shapes=[
            pltpu.VMEM((23, slots, 32, 128), F32),
            pltpu.VMEM((22 * slots * JP, PAIR), BF16),
        ]
        + back
        + [pltpu.VMEM((SIDE, slots, JP, C), F32)],
        compiler_params=pltpu.CompilerParams(vmem_limit_bytes=LIMIT),
        cost_estimate=cost(3 * one_product),
        name="first_pass",
    )(
        tissue_rows,
        filters.T,
        arranged(image_stack, C),
        arranged(codes_start, M),
        arranged(duals_start, M),
    )
    everyone = lax.all_gather(payload, "tile", axis=0)
    codes, duals = pl.pallas_call(
        second_kernel,
        out_shape=(state, state),
        in_specs=[in_vmem()] * 4,
        out_specs=(in_vmem(),) * 2,
        scratch_shapes=back,
        compiler_params=pltpu.CompilerParams(vmem_limit_bytes=LIMIT),
        cost_estimate=cost(one_product),
        name="second_codes",
    )(filters.T, payload, codes_mid, duals_mid)
    group = 8
    columns = filters.T
    new_filters = pl.pallas_call(
        lambda *refs: dictionary_kernel(stride, *refs),
        grid=(groups // group,),
        out_shape=jax.ShapeDtypeStruct((COLS, C), BF16),
        in_specs=[
            pl.BlockSpec((COLS, C), lambda g: (0, 0), pipeline_mode=pl.Buffered(1)),
            pl.BlockSpec((group, SIDE, slots, JP, C), lambda g: (g, 0, 0, 0, 0)),
        ],
        out_specs=pl.BlockSpec((COLS, C), lambda g: (0, 0), pipeline_mode=pl.Buffered(1)),
        scratch_shapes=[
            pltpu.VMEM((SIDE, group, JP, M), F32),
            pltpu.VMEM((LAST, 22 * group * JP), BF16),
            pltpu.VMEM((SIDE, group, JP, C), F32),
            pltpu.VMEM((COLS, C), F32),
        ],
        compiler_params=pltpu.CompilerParams(vmem_limit_bytes=LIMIT),
        cost_estimate=cost(groups * one_product // 2),
        name="dictionary",
    )(columns, everyone)

    def flat(array):
        return array[:, :, 0:SIDE, :].transpose(1, 0, 2, 3).reshape(slots, SIDE * SIDE * M)

    return flat(codes), flat(duals), new_filters.T


def solution(mesh):
    return jax.shard_map(
        local,
        mesh=mesh,
        in_specs=(
            P(("runs", "tile"), None, None),
            P(("runs", "tile")),
            P(),
            P(("runs", "tile"), None),
            P(("runs", "tile"), None),
        ),
        out_specs=(P(("runs", "tile"), None), P(("runs", "tile"), None), P("runs", None)),
        check_vma=False,
    )
```

```python
import math

import jax
import jax.numpy as jnp
from jax import lax
from jax.experimental import pallas as pl
from jax.experimental.pallas import tpu as pltpu
from jax.sharding import PartitionSpec as P

M = 64
C = 256
K = 11
SIDE = 12
JP = 16
PAIR = 2 * K * M
LAST = K * M
COLS = K * K * M
BLOCKS = PAIR // 128
FACTOR = 1.0 / math.sqrt(K * K * M)

PENALTY = 10.0
SPARSITY = 2.0
EPSILON = 1e-05
RELAX = 1.8

F32 = jnp.float32
BF16 = jnp.bfloat16


def put_codes(dpad, codes):
    both = jnp.concatenate([codes, codes], axis=-1)
    dpad[5 : 5 + SIDE, :, 6 : 6 + SIDE, 0:M] = both[..., 0:M]
    dpad[5 : 5 + SIDE, :, 5 : 5 + SIDE, M : 2 * M] = both[..., M : 2 * M]


def build_taps(dpad, taps):
    slots = dpad.shape[1]
    rows = 22 * slots * JP
    for q in range(BLOCKS):
        if q < 5:
            block = dpad[0:22, :, 2 * q + 1 : 2 * q + 1 + JP, :]
        elif q > 5:
            start = 2 * (q - 6) + 2
            block = dpad[1:23, :, start : start + JP, :]
        else:
            low = dpad[0:22, :, 11 : 11 + JP, :]
            high = dpad[1:23, :, 0:JP, :]
            lane = lax.broadcasted_iota(jnp.int32, low.shape, 3)
            block = jnp.where(lane < M, low, high)
        taps[:, q * 128 : (q + 1) * 128] = block.reshape(rows, 128).astype(BF16)


def rebuild(taps, f_ref, slots):
    rows = SIDE * slots * JP
    total = None
    for p in range(6):
        width = PAIR if p < 5 else LAST
        at = p * 2 * slots * JP
        part = lax.dot_general(
            taps[at : at + rows, 0:width],
            f_ref[p * PAIR : p * PAIR + width, :],
            (((1,), (0,)), ((), ())),
            preferred_element_type=F32,
        )
        total = part if total is None else total + part
    return total


def fill_tail(f_ref, ftail):
    ftail[...] = jnp.zeros_like(ftail)
    ftail[0:192, :] = f_ref[COLS - 192 : COLS, :]


def code_gradient(rpad, f_ref, ftail, zpad, slots):
    rows = 13 * slots * JP
    step = slots * JP
    for n in range(6):
        width = 256 if n < 5 else 128
        acc = None
        for p in range(6):
            at = (10 - 2 * p) * step
            if p < 5 or n < 2:
                piece = f_ref[p * PAIR + n * 256 : p * PAIR + n * 256 + width, :]
            elif n == 2:
                piece = ftail[...]
            else:
                continue
            part = lax.dot_general(
                rpad[at : at + rows, :],
                piece,
                (((1,), (1,)), ((), ())),
                preferred_element_type=F32,
            )
            acc = part if acc is None else acc + part
        for h in range(width // 128):
            zpad[2 * n + h, :, :, 8:24, :] = acc[:, h * 128 : (h + 1) * 128].reshape(
                13, slots, JP, 128
            )
    total = None
    for q in range(BLOCKS):
        if q < 5:
            part = zpad[q, 1:13, :, 12 - 2 * q : 36 - 2 * q, :]
        elif q > 5:
            start = 11 - 2 * (q - 6)
            part = zpad[q, 0:12, :, start : start + 24, :]
        else:
            low = zpad[q, 1:13, :, 2:26, :]
            high = zpad[q, 0:12, :, 13:37, :]
            lane = lax.broadcasted_iota(jnp.int32, low.shape, 3)
            part = jnp.where(lane < M, low, high)
        total = part if total is None else total + part
    zpad[0, 0:12, :, 0:24, :] = total
    low = zpad[0, 0:12, :, 1 : 1 + JP, 0:M]
    high = zpad[0, 0:12, :, 0:JP, M : 2 * M]
    return (low + high) * FACTOR


def admm_update(codes_now, duals_now, gradient):
    primal = codes_now - duals_now - gradient / PENALTY
    relaxed = RELAX * primal + (1.0 - RELAX) * codes_now
    merged = relaxed + duals_now
    level = SPARSITY / PENALTY
    shrunk = jnp.where(
        merged > level, merged - level, jnp.where(merged < -level, merged + level, 0.0)
    )
    return shrunk, duals_now + relaxed - shrunk


def tissue_of(rows_ref, shape):
    row = lax.broadcasted_iota(jnp.int32, shape, 0)
    slot = lax.broadcasted_iota(jnp.int32, shape, 1)
    col = lax.broadcasted_iota(jnp.int32, shape, 2)
    height = jnp.full(shape, 0, jnp.int32)
    for s in range(shape[1]):
        height = jnp.where(slot == s, rows_ref[s], height)
    return (row < height) & (col < SIDE), height > 0


def first_kernel(
    rows_ref, f_ref, img_ref, codes_ref, duals_ref, pay_ref, codes_out, duals_out,
    dpad, taps, rpad, ftail, zpad, stage
):
    slots = img_ref.shape[1]
    rows = SIDE * slots * JP
    lead = 6 * slots * JP
    dpad[...] = jnp.zeros_like(dpad)
    rpad[...] = jnp.zeros_like(rpad)
    zpad[...] = jnp.zeros_like(zpad)
    fill_tail(f_ref, ftail)
    inside, occupied = tissue_of(rows_ref, (SIDE, slots, JP, C))
    codes = codes_ref[...].astype(F32)
    duals = duals_ref[...].astype(F32)
    images = img_ref[...].astype(F32)

    def residual_of(values):
        put_codes(dpad, values[:, :, 0:SIDE, :])
        build_taps(dpad, taps)
        rebuilt = rebuild(taps, f_ref, slots).reshape(SIDE, slots, JP, C) * FACTOR
        return jnp.where(inside, rebuilt - images, 0.0)

    residual = residual_of(codes)
    rpad[lead : lead + rows, :] = residual.reshape(rows, C).astype(BF16)
    gradient = code_gradient(rpad, f_ref, ftail, zpad, slots)
    codes, duals = admm_update(codes, duals, gradient)
    codes_out[...] = codes
    duals_out[...] = duals
    residual = residual_of(codes)
    stage[...] = residual
    held = jnp.where(occupied[..., 0:M], codes, 0.0)
    for k in range(3):
        stage[:, :, SIDE:JP, k * M : (k + 1) * M] = held[:, :, 4 * k : 4 * k + 4, :]
    for s in range(slots):
        pay_ref[s] = stage[:, s, :, :].astype(BF16)


def second_kernel(f_ref, pay_ref, codes_ref, duals_ref, codes_out, duals_out, rpad, ftail, zpad):
    slots = pay_ref.shape[0]
    rpad[...] = jnp.zeros_like(rpad)
    zpad[...] = jnp.zeros_like(zpad)
    fill_tail(f_ref, ftail)
    for s in range(slots):
        payload = pay_ref[s].astype(F32)
        col = lax.broadcasted_iota(jnp.int32, payload.shape, 1)
        residual = jnp.where(col < SIDE, payload, 0.0).astype(BF16)
        for i in range(SIDE):
            at = ((6 + i) * slots + s) * JP
            rpad[at : at + JP, :] = residual[i]
    gradient = code_gradient(rpad, f_ref, ftail, zpad, slots)
    codes, duals = admm_update(codes_ref[...], duals_ref[...], gradient)
    codes_out[...] = codes
    duals_out[...] = duals


MESH = pl.DeviceIdType.MESH


def gather_kernel(
    outer, inner, pay_ref, all_ref, other, pair_send, pair_recv, z_send, z_recv,
    y_send, y_recv, c_send, c_recv
):
    me = lax.axis_index("tile")
    core = lax.rem(me, 2)
    inn = lax.rem(me // 2, inner)
    out = me // (2 * inner)

    def index(dz, dy, c):
        return (lax.rem(out + dz + outer, outer) * inner + lax.rem(inn + dy + inner, inner)) * 2 + c

    partner = index(0, 0, 1 - core)
    barrier = pltpu.get_barrier_semaphore()
    peers = [index(dz, 0, core) for dz in range(1, outer)]
    peers += [index(0, dy, core) for dy in range(1, inner)] + [partner]
    for peer in peers:
        pl.semaphore_signal(barrier, inc=1, device_id={"tile": peer}, device_id_type=MESH)
    pl.semaphore_wait(barrier, len(peers))

    def copy(src, dst, send, recv, target):
        return pltpu.make_async_remote_copy(
            src_ref=src,
            dst_ref=dst,
            send_sem=send,
            recv_sem=recv,
            device_id={"tile": target},
            device_id_type=MESH,
        )

    swap = copy(pay_ref.at[1], other, pair_send, pair_recv, partner)
    swap.start()
    swap.wait()
    all_ref[me] = (pay_ref[0].astype(F32) + other[...].astype(F32)).astype(BF16)

    started = []

    def along_z(dz):
        return copy(all_ref.at[me], all_ref.at[me], z_send.at[dz], z_recv.at[dz], index(dz, 0, core))

    def along_y(dz, dy):
        block = all_ref.at[index(-dz, 0, core)]
        return copy(block, block, y_send.at[dz, dy], y_recv.at[dz, dy], index(0, dy, core))

    def across(dz, dy):
        block = all_ref.at[index(-dz, -dy, core)]
        return copy(block, block, c_send.at[dz, dy], c_recv.at[dz, dy], partner)

    def start(one):
        one.start()
        started.append(one)

    def arrived(block, recv, send):
        copy(block, block, send, recv, partner).wait_recv()

    for dz in range(1, outer):
        start(along_z(dz))
    for dy in range(1, inner):
        start(along_y(0, dy))
    start(across(0, 0))
    for dz in range(1, outer):
        arrived(all_ref.at[index(-dz, 0, core)], z_recv.at[dz], z_send.at[dz])
        for dy in range(1, inner):
            start(along_y(dz, dy))
        start(across(dz, 0))
    for dz in range(outer):
        for dy in range(1, inner):
            arrived(all_ref.at[index(-dz, -dy, core)], y_recv.at[dz, dy], y_send.at[dz, dy])
            start(across(dz, dy))
    for dz in range(outer):
        for dy in range(inner):
            arrived(all_ref.at[index(-dz, -dy, 1 - core)], c_recv.at[dz, dy], c_send.at[dz, dy])
    for one in started:
        one.wait_send()


def dictionary_kernel(stride, f_ref, all_ref, new_ref, maps, taps, stage, total):
    at = pl.program_id(0)
    group = all_ref.shape[0]
    row = group * JP
    rows = SIDE * row
    edge = (K - 1) // 2

    @pl.when(at == 0)
    def _():
        maps[...] = jnp.zeros_like(maps)
        taps[...] = jnp.zeros_like(taps)
        total[...] = jnp.zeros_like(total)

    for d in range(group):
        stage[:, d, :, :] = all_ref[d].astype(F32)
    for k in range(3):
        maps[:, :, 4 * k : 4 * k + 4, :] = stage[:, :, SIDE:JP, k * M : (k + 1) * M]
    col = lax.broadcasted_iota(jnp.int32, (M, row), 1) % JP
    for i in range(SIDE):
        turned = maps[i].reshape(row, M).T
        for b in range(K):
            moved = turned if b == edge else pltpu.roll(turned, (edge - b) % row, 1)
            if b == 0:
                moved = jnp.where(col == 0, 0.0, moved)
            if b == K - 1:
                moved = jnp.where(col == SIDE - 1, 0.0, moved)
            taps[b * M : (b + 1) * M, (i + edge) * row : (i + edge + 1) * row] = moved.astype(BF16)
    values = stage[...]
    place = lax.broadcasted_iota(jnp.int32, values.shape, 2)
    residual = jnp.where(place < SIDE, values, 0.0).reshape(rows, C).astype(BF16)
    for a in range(K):
        total[a * LAST : (a + 1) * LAST, :] += jnp.dot(
            taps[:, a * row : a * row + rows], residual, preferred_element_type=F32
        )

    @pl.when(at == pl.num_programs(0) - 1)
    def _():
        def step(t, squares):
            part = pl.ds(pl.multiple_of(t * M, M), M)
            moved = f_ref[part, :].astype(F32) - (stride * FACTOR) * total[part, :]
            total[part, :] = moved
            return squares + moved * moved

        squares = lax.fori_loop(0, K * K, step, jnp.zeros((M, C), F32), unroll=11)
        sums = jnp.sum(squares, axis=1, keepdims=True)
        inverse = 1.0 / jnp.sqrt(sums / (C * K * K) + EPSILON)

        def scale(t, carry):
            part = pl.ds(pl.multiple_of(t * M, M), M)
            new_ref[part, :] = (total[part, :] * inverse).astype(BF16)
            return carry

        lax.fori_loop(0, K * K, scale, 0, unroll=11)


def in_vmem():
    return pl.BlockSpec(memory_space=pltpu.VMEM)


LIMIT = 56 * 1024 * 1024


def cost(flops):
    return pl.CostEstimate(flops=flops, bytes_accessed=8 * 1024 * 1024, transcendentals=0)


def local(image_stack, tissue_rows, filters, codes_start, duals_start):
    slots = image_stack.shape[0]
    groups = lax.axis_size("tile")
    stride = 0.5 * math.sqrt(COLS / (SIDE * SIDE * slots * groups))

    def arranged(array, width):
        shaped = array.reshape(slots, SIDE, SIDE, width).transpose(1, 0, 2, 3)
        return jnp.pad(shaped, ((0, 0), (0, 0), (0, JP - SIDE), (0, 0)))

    state = jax.ShapeDtypeStruct((SIDE, slots, JP, M), F32)
    one_product = 2 * SIDE * SIDE * slots * C * COLS
    back = [
        pltpu.VMEM((23 * slots * JP, C), BF16),
        pltpu.VMEM((256, C), BF16),
        pltpu.VMEM((BLOCKS, 13, slots, 40, 128), F32),
    ]
    payload, codes_mid, duals_mid = pl.pallas_call(
        first_kernel,
        out_shape=(jax.ShapeDtypeStruct((slots, SIDE, JP, C), BF16), state, state),
        in_specs=[pl.BlockSpec(memory_space=pltpu.SMEM)] + [in_vmem()] * 4,
        out_specs=(in_vmem(),) * 3,
        scratch_shapes=[
            pltpu.VMEM((23, slots, 32, 128), F32),
            pltpu.VMEM((22 * slots * JP, PAIR), BF16),
        ]
        + back
        + [pltpu.VMEM((SIDE, slots, JP, C), F32)],
        compiler_params=pltpu.CompilerParams(vmem_limit_bytes=LIMIT),
        cost_estimate=cost(3 * one_product),
        name="first_pass",
    )(
        tissue_rows,
        filters.T,
        arranged(image_stack, C),
        arranged(codes_start, M),
        arranged(duals_start, M),
    )
    chips = groups // 2
    inner = 1 << ((chips.bit_length() - 1) // 2)
    outer = chips // inner
    dma = pltpu.SemaphoreType.DMA
    everyone = pl.pallas_call(
        lambda *refs: gather_kernel(outer, inner, *refs),
        out_shape=jax.ShapeDtypeStruct((groups, SIDE, JP, C), BF16),
        in_specs=[in_vmem()],
        out_specs=in_vmem(),
        scratch_shapes=[
            pltpu.VMEM((SIDE, JP, C), BF16),
            dma,
            dma,
            dma((outer,)),
            dma((outer,)),
            dma((outer, inner)),
            dma((outer, inner)),
            dma((outer, inner)),
            dma((outer, inner)),
        ],
        compiler_params=pltpu.CompilerParams(
            vmem_limit_bytes=LIMIT, collective_id=0, has_side_effects=True
        ),
        cost_estimate=cost(1),
        name="gather_slots",
    )(payload)
    codes, duals = pl.pallas_call(
        second_kernel,
        out_shape=(state, state),
        in_specs=[in_vmem()] * 4,
        out_specs=(in_vmem(),) * 2,
        scratch_shapes=back,
        compiler_params=pltpu.CompilerParams(vmem_limit_bytes=LIMIT),
        cost_estimate=cost(one_product),
        name="second_codes",
    )(filters.T, payload, codes_mid, duals_mid)
    group = 8
    columns = filters.T
    new_filters = pl.pallas_call(
        lambda *refs: dictionary_kernel(stride, *refs),
        grid=(groups // group,),
        out_shape=jax.ShapeDtypeStruct((COLS, C), BF16),
        in_specs=[
            pl.BlockSpec((COLS, C), lambda g: (0, 0), pipeline_mode=pl.Buffered(1)),
            pl.BlockSpec((group, SIDE, JP, C), lambda g: (g, 0, 0, 0)),
        ],
        out_specs=pl.BlockSpec((COLS, C), lambda g: (0, 0), pipeline_mode=pl.Buffered(1)),
        scratch_shapes=[
            pltpu.VMEM((SIDE, group, JP, M), F32),
            pltpu.VMEM((LAST, 22 * group * JP), BF16),
            pltpu.VMEM((SIDE, group, JP, C), F32),
            pltpu.VMEM((COLS, C), F32),
        ],
        compiler_params=pltpu.CompilerParams(vmem_limit_bytes=LIMIT),
        cost_estimate=cost(groups * one_product // 2),
        name="dictionary",
    )(columns, everyone)

    def flat(array):
        return array[:, :, 0:SIDE, :].transpose(1, 0, 2, 3).reshape(slots, SIDE * SIDE * M)

    return flat(codes), flat(duals), new_filters.T


def solution(mesh):
    return jax.shard_map(
        local,
        mesh=mesh,
        in_specs=(
            P(("runs", "tile"), None, None),
            P(("runs", "tile")),
            P(),
            P(("runs", "tile"), None),
            P(("runs", "tile"), None),
        ),
        out_specs=(P(("runs", "tile"), None), P(("runs", "tile"), None), P("runs", None)),
        check_vma=False,
    )
```

```python
import math

import jax
import jax.numpy as jnp
from jax import lax
from jax.experimental import pallas as pl
from jax.experimental.pallas import tpu as pltpu
from jax.sharding import PartitionSpec as P

M = 64
C = 256
K = 11
SIDE = 12
JP = 16
PAIR = 2 * K * M
LAST = K * M
COLS = K * K * M
BLOCKS = PAIR // 128
FACTOR = 1.0 / math.sqrt(K * K * M)

PENALTY = 10.0
SPARSITY = 2.0
EPSILON = 1e-05
RELAX = 1.8

F32 = jnp.float32
BF16 = jnp.bfloat16


def put_codes(dpad, codes):
    both = jnp.concatenate([codes, codes], axis=-1)
    dpad[5 : 5 + SIDE, :, 6 : 6 + SIDE, 0:M] = both[..., 0:M]
    dpad[5 : 5 + SIDE, :, 5 : 5 + SIDE, M : 2 * M] = both[..., M : 2 * M]


def build_taps(dpad, taps):
    slots = dpad.shape[1]
    rows = 22 * slots * JP
    for q in range(BLOCKS):
        if q < 5:
            block = dpad[0:22, :, 2 * q + 1 : 2 * q + 1 + JP, :]
        elif q > 5:
            start = 2 * (q - 6) + 2
            block = dpad[1:23, :, start : start + JP, :]
        else:
            low = dpad[0:22, :, 11 : 11 + JP, :]
            high = dpad[1:23, :, 0:JP, :]
            lane = lax.broadcasted_iota(jnp.int32, low.shape, 3)
            block = jnp.where(lane < M, low, high)
        taps[:, q * 128 : (q + 1) * 128] = block.reshape(rows, 128).astype(BF16)


def rebuild(taps, f_ref, slots):
    rows = SIDE * slots * JP
    total = None
    for p in range(6):
        width = PAIR if p < 5 else LAST
        at = p * 2 * slots * JP
        part = lax.dot_general(
            taps[at : at + rows, 0:width],
            f_ref[p * PAIR : p * PAIR + width, :],
            (((1,), (0,)), ((), ())),
            preferred_element_type=F32,
        )
        total = part if total is None else total + part
    return total


def fill_tail(f_ref, ftail):
    ftail[...] = jnp.zeros_like(ftail)
    ftail[0:192, :] = f_ref[COLS - 192 : COLS, :]


def code_gradient(rpad, f_ref, ftail, zpad, slots):
    rows = 13 * slots * JP
    step = slots * JP
    for n in range(6):
        width = 256 if n < 5 else 128
        acc = None
        for p in range(6):
            at = (10 - 2 * p) * step
            if p < 5 or n < 2:
                piece = f_ref[p * PAIR + n * 256 : p * PAIR + n * 256 + width, :]
            elif n == 2:
                piece = ftail[...]
            else:
                continue
            part = lax.dot_general(
                rpad[at : at + rows, :],
                piece,
                (((1,), (1,)), ((), ())),
                preferred_element_type=F32,
            )
            acc = part if acc is None else acc + part
        for h in range(width // 128):
            zpad[2 * n + h, :, :, 8:24, :] = acc[:, h * 128 : (h + 1) * 128].reshape(
                13, slots, JP, 128
            )
    total = None
    for q in range(BLOCKS):
        if q < 5:
            part = zpad[q, 1:13, :, 12 - 2 * q : 36 - 2 * q, :]
        elif q > 5:
            start = 11 - 2 * (q - 6)
            part = zpad[q, 0:12, :, start : start + 24, :]
        else:
            low = zpad[q, 1:13, :, 2:26, :]
            high = zpad[q, 0:12, :, 13:37, :]
            lane = lax.broadcasted_iota(jnp.int32, low.shape, 3)
            part = jnp.where(lane < M, low, high)
        total = part if total is None else total + part
    zpad[0, 0:12, :, 0:24, :] = total
    low = zpad[0, 0:12, :, 1 : 1 + JP, 0:M]
    high = zpad[0, 0:12, :, 0:JP, M : 2 * M]
    return (low + high) * FACTOR


def admm_update(codes_now, duals_now, gradient):
    primal = codes_now - duals_now - gradient / PENALTY
    relaxed = RELAX * primal + (1.0 - RELAX) * codes_now
    merged = relaxed + duals_now
    level = SPARSITY / PENALTY
    shrunk = jnp.where(
        merged > level, merged - level, jnp.where(merged < -level, merged + level, 0.0)
    )
    return shrunk, duals_now + relaxed - shrunk


def tissue_of(rows_ref, shape):
    row = lax.broadcasted_iota(jnp.int32, shape, 0)
    slot = lax.broadcasted_iota(jnp.int32, shape, 1)
    col = lax.broadcasted_iota(jnp.int32, shape, 2)
    height = jnp.full(shape, 0, jnp.int32)
    for s in range(shape[1]):
        height = jnp.where(slot == s, rows_ref[s], height)
    return (row < height) & (col < SIDE), height > 0


def first_kernel(
    rows_ref, f_ref, img_ref, codes_ref, duals_ref, pay_ref, codes_out, duals_out,
    dpad, taps, rpad, ftail, zpad, stage
):
    slots = img_ref.shape[1]
    rows = SIDE * slots * JP
    lead = 6 * slots * JP
    dpad[...] = jnp.zeros_like(dpad)
    rpad[...] = jnp.zeros_like(rpad)
    zpad[...] = jnp.zeros_like(zpad)
    fill_tail(f_ref, ftail)
    inside, occupied = tissue_of(rows_ref, (SIDE, slots, JP, C))
    codes = codes_ref[...].astype(F32)
    duals = duals_ref[...].astype(F32)
    images = img_ref[...].astype(F32)

    def residual_of(values):
        put_codes(dpad, values[:, :, 0:SIDE, :])
        build_taps(dpad, taps)
        rebuilt = rebuild(taps, f_ref, slots).reshape(SIDE, slots, JP, C) * FACTOR
        return jnp.where(inside, rebuilt - images, 0.0)

    residual = residual_of(codes)
    rpad[lead : lead + rows, :] = residual.reshape(rows, C).astype(BF16)
    gradient = code_gradient(rpad, f_ref, ftail, zpad, slots)
    codes, duals = admm_update(codes, duals, gradient)
    codes_out[...] = codes
    duals_out[...] = duals
    residual = residual_of(codes)
    stage[...] = residual
    held = jnp.where(occupied[..., 0:M], codes, 0.0)
    for k in range(3):
        stage[:, :, SIDE:JP, k * M : (k + 1) * M] = held[:, :, 4 * k : 4 * k + 4, :]
    for s in range(slots):
        pay_ref[s] = stage[:, s, :, :].astype(BF16)


def second_codes(f_ref, pay_ref, codes_ref, duals_ref, codes_out, duals_out, rpad, ftail, zpad):
    slots = pay_ref.shape[0]
    rpad[...] = jnp.zeros_like(rpad)
    zpad[...] = jnp.zeros_like(zpad)
    fill_tail(f_ref, ftail)
    for s in range(slots):
        payload = pay_ref[s].astype(F32)
        col = lax.broadcasted_iota(jnp.int32, payload.shape, 1)
        residual = jnp.where(col < SIDE, payload, 0.0).astype(BF16)
        for i in range(SIDE):
            at = ((6 + i) * slots + s) * JP
            rpad[at : at + JP, :] = residual[i]
    gradient = code_gradient(rpad, f_ref, ftail, zpad, slots)
    codes, duals = admm_update(codes_ref[...], duals_ref[...], gradient)
    codes_out[...] = codes
    duals_out[...] = duals


MESH = pl.DeviceIdType.MESH


def gather_kernel(
    outer, inner, f_ref, pay_ref, codes_ref, duals_ref, all_ref, codes_out, duals_out,
    rpad, ftail, zpad, other, pair_send, pair_recv, z_send, z_recv,
    y_send, y_recv, c_send, c_recv
):
    me = lax.axis_index("tile")
    core = lax.rem(me, 2)
    inn = lax.rem(me // 2, inner)
    out = me // (2 * inner)

    def index(dz, dy, c):
        return (lax.rem(out + dz + outer, outer) * inner + lax.rem(inn + dy + inner, inner)) * 2 + c

    partner = index(0, 0, 1 - core)
    barrier = pltpu.get_barrier_semaphore()
    peers = [index(dz, 0, core) for dz in range(1, outer)]
    peers += [index(0, dy, core) for dy in range(1, inner)] + [partner]
    for peer in peers:
        pl.semaphore_signal(barrier, inc=1, device_id={"tile": peer}, device_id_type=MESH)
    pl.semaphore_wait(barrier, len(peers))

    def copy(src, dst, send, recv, target):
        return pltpu.make_async_remote_copy(
            src_ref=src,
            dst_ref=dst,
            send_sem=send,
            recv_sem=recv,
            device_id={"tile": target},
            device_id_type=MESH,
        )

    swap = copy(pay_ref.at[1], other, pair_send, pair_recv, partner)
    swap.start()
    swap.wait()
    all_ref[me] = (pay_ref[0].astype(F32) + other[...].astype(F32)).astype(BF16)

    started = []

    def along_z(dz):
        return copy(all_ref.at[me], all_ref.at[me], z_send.at[dz], z_recv.at[dz], index(dz, 0, core))

    def along_y(dz, dy):
        block = all_ref.at[index(-dz, 0, core)]
        return copy(block, block, y_send.at[dz, dy], y_recv.at[dz, dy], index(0, dy, core))

    def across(dz, dy):
        block = all_ref.at[index(-dz, -dy, core)]
        return copy(block, block, c_send.at[dz, dy], c_recv.at[dz, dy], partner)

    def start(one):
        one.start()
        started.append(one)

    def arrived(block, recv, send):
        copy(block, block, send, recv, partner).wait_recv()

    for dz in range(1, outer):
        start(along_z(dz))
    for dy in range(1, inner):
        start(along_y(0, dy))
    start(across(0, 0))
    second_codes(f_ref, pay_ref, codes_ref, duals_ref, codes_out, duals_out, rpad, ftail, zpad)
    for dz in range(1, outer):
        arrived(all_ref.at[index(-dz, 0, core)], z_recv.at[dz], z_send.at[dz])
        for dy in range(1, inner):
            start(along_y(dz, dy))
        start(across(dz, 0))
    for dz in range(outer):
        for dy in range(1, inner):
            arrived(all_ref.at[index(-dz, -dy, core)], y_recv.at[dz, dy], y_send.at[dz, dy])
            start(across(dz, dy))
    for dz in range(outer):
        for dy in range(inner):
            arrived(all_ref.at[index(-dz, -dy, 1 - core)], c_recv.at[dz, dy], c_send.at[dz, dy])
    for one in started:
        one.wait_send()


def dictionary_kernel(stride, steps, f_hbm, all_ref, new_hbm, maps, taps, stage, total, f_ref, new_ref, f_sem, new_sem):
    at = pl.program_id(0)
    fetch = pltpu.make_async_copy(f_hbm, f_ref, f_sem)
    group = all_ref.shape[0]
    row = group * JP
    rows = SIDE * row
    edge = (K - 1) // 2

    @pl.when(at == 0)
    def _():
        fetch.start()
        maps[...] = jnp.zeros_like(maps)
        taps[...] = jnp.zeros_like(taps)
        if steps > 1:
            total[...] = jnp.zeros_like(total)

    for d in range(group):
        stage[:, d, :, :] = all_ref[d].astype(F32)
    for k in range(3):
        maps[:, :, 4 * k : 4 * k + 4, :] = stage[:, :, SIDE:JP, k * M : (k + 1) * M]
    col = lax.broadcasted_iota(jnp.int32, (M, row), 1) % JP
    for i in range(SIDE):
        turned = maps[i].reshape(row, M).T
        for b in range(K):
            moved = turned if b == edge else pltpu.roll(turned, (edge - b) % row, 1)
            if b == 0:
                moved = jnp.where(col == 0, 0.0, moved)
            if b == K - 1:
                moved = jnp.where(col == SIDE - 1, 0.0, moved)
            taps[b * M : (b + 1) * M, (i + edge) * row : (i + edge + 1) * row] = moved.astype(BF16)
    values = stage[...]
    place = lax.broadcasted_iota(jnp.int32, values.shape, 2)
    residual = jnp.where(place < SIDE, values, 0.0).reshape(rows, C).astype(BF16)
    @pl.when(at == 0)
    def _():
        fetch.wait()

    def term(a):
        return jnp.dot(
            taps[:, a * row : a * row + rows], residual, preferred_element_type=F32
        )

    def finish(part, summed):
        return f_ref[part, :].astype(F32) - (stride * FACTOR) * summed

    def close(squares):
        sums = jnp.sum(squares, axis=1, keepdims=True)
        inverse = 1.0 / jnp.sqrt(sums / (C * K * K) + EPSILON)
        inverse = jnp.broadcast_to(inverse, (M, C))
        sends = []
        for a in range(K):
            part = slice(a * LAST, (a + 1) * LAST)
            values = total[part, :].reshape(K, M, C) * inverse[None]
            new_ref[part, :] = values.reshape(LAST, C).astype(BF16)
            send = pltpu.make_async_copy(new_ref.at[part], new_hbm.at[part], new_sem.at[a])
            send.start()
            sends.append(send)
        for send in sends:
            send.wait()

    if steps == 1:
        squares = jnp.zeros((M, C), F32)
        for a in range(K):
            part = slice(a * LAST, (a + 1) * LAST)
            moved = finish(part, term(a))
            total[part, :] = moved
            squares = squares + jnp.sum((moved * moved).reshape(K, M, C), axis=0)
        close(squares)
        return

    for a in range(K):
        total[a * LAST : (a + 1) * LAST, :] += term(a)

    @pl.when(at == steps - 1)
    def _():
        squares = jnp.zeros((M, C), F32)
        for a in range(K):
            part = slice(a * LAST, (a + 1) * LAST)
            moved = finish(part, total[part, :])
            total[part, :] = moved
            squares = squares + jnp.sum((moved * moved).reshape(K, M, C), axis=0)
        close(squares)


def in_vmem():
    return pl.BlockSpec(memory_space=pltpu.VMEM)


LIMIT = 56 * 1024 * 1024


def cost(flops):
    return pl.CostEstimate(flops=flops, bytes_accessed=8 * 1024 * 1024, transcendentals=0)


def local(image_stack, tissue_rows, filters, codes_start, duals_start):
    slots = image_stack.shape[0]
    groups = lax.axis_size("tile")
    stride = 0.5 * math.sqrt(COLS / (SIDE * SIDE * slots * groups))

    def arranged(array, width):
        shaped = array.reshape(slots, SIDE, SIDE, width).transpose(1, 0, 2, 3)
        return jnp.pad(shaped, ((0, 0), (0, 0), (0, JP - SIDE), (0, 0)))

    state = jax.ShapeDtypeStruct((SIDE, slots, JP, M), F32)
    one_product = 2 * SIDE * SIDE * slots * C * COLS
    back = [
        pltpu.VMEM((23 * slots * JP, C), BF16),
        pltpu.VMEM((256, C), BF16),
        pltpu.VMEM((BLOCKS, 13, slots, 40, 128), F32),
    ]
    payload, codes_mid, duals_mid = pl.pallas_call(
        first_kernel,
        out_shape=(jax.ShapeDtypeStruct((slots, SIDE, JP, C), BF16), state, state),
        in_specs=[pl.BlockSpec(memory_space=pltpu.SMEM)] + [in_vmem()] * 4,
        out_specs=(in_vmem(),) * 3,
        scratch_shapes=[
            pltpu.VMEM((23, slots, 32, 128), F32),
            pltpu.VMEM((22 * slots * JP, PAIR), BF16),
        ]
        + back
        + [pltpu.VMEM((SIDE, slots, JP, C), F32)],
        compiler_params=pltpu.CompilerParams(vmem_limit_bytes=LIMIT),
        cost_estimate=cost(3 * one_product),
        name="first_pass",
    )(
        tissue_rows,
        filters.T,
        arranged(image_stack, C),
        arranged(codes_start, M),
        arranged(duals_start, M),
    )
    chips = groups // 2
    inner = 1 << ((chips.bit_length() - 1) // 2)
    outer = chips // inner
    dma = pltpu.SemaphoreType.DMA
    everyone, codes, duals = pl.pallas_call(
        lambda *refs: gather_kernel(outer, inner, *refs),
        out_shape=(jax.ShapeDtypeStruct((groups, SIDE, JP, C), BF16), state, state),
        in_specs=[in_vmem()] * 4,
        out_specs=(in_vmem(),) * 3,
        scratch_shapes=back
        + [
            pltpu.VMEM((SIDE, JP, C), BF16),
            dma,
            dma,
            dma((outer,)),
            dma((outer,)),
            dma((outer, inner)),
            dma((outer, inner)),
            dma((outer, inner)),
            dma((outer, inner)),
        ],
        compiler_params=pltpu.CompilerParams(
            vmem_limit_bytes=LIMIT, collective_id=0, has_side_effects=True
        ),
        cost_estimate=cost(one_product),
        name="gather_slots",
    )(filters.T, payload, codes_mid, duals_mid)
    group = 16 if groups % 16 == 0 else 8
    steps = groups // group
    columns = filters.T
    new_filters = pl.pallas_call(
        lambda *refs: dictionary_kernel(stride, steps, *refs),
        grid=(steps,),
        out_shape=jax.ShapeDtypeStruct((COLS, C), BF16),
        in_specs=[
            pl.BlockSpec(memory_space=pl.ANY),
            pl.BlockSpec((group, SIDE, JP, C), lambda g: (g, 0, 0, 0)),
        ],
        out_specs=pl.BlockSpec(memory_space=pl.ANY),
        scratch_shapes=[
            pltpu.VMEM((SIDE, group, JP, M), F32),
            pltpu.VMEM((LAST, 22 * group * JP), BF16),
            pltpu.VMEM((SIDE, group, JP, C), F32),
            pltpu.VMEM((COLS, C), F32),
            pltpu.VMEM((COLS, C), BF16),
            pltpu.VMEM((COLS, C), BF16),
            dma,
            dma((K,)),
        ],
        compiler_params=pltpu.CompilerParams(vmem_limit_bytes=LIMIT),
        cost_estimate=cost(groups * one_product // 2),
        name="dictionary",
    )(columns, everyone)

    def flat(array):
        return array[:, :, 0:SIDE, :].transpose(1, 0, 2, 3).reshape(slots, SIDE * SIDE * M)

    return flat(codes), flat(duals), new_filters.T


def solution(mesh):
    return jax.shard_map(
        local,
        mesh=mesh,
        in_specs=(
            P(("runs", "tile"), None, None),
            P(("runs", "tile")),
            P(),
            P(("runs", "tile"), None),
            P(("runs", "tile"), None),
        ),
        out_specs=(P(("runs", "tile"), None), P(("runs", "tile"), None), P("runs", None)),
        check_vma=False,
    )
```
